32 devices in a mesh: dp: 8 (over y, x, core), tensor: 4 (over z).
Axes of the slice: x: 2, y: 2, z: 4, core: 2. Of those that a mesh axis runs over, the one named last changes fastest.
Arguments:
- latents: bfloat16 [16, 256, 768], P('dp'), may hold values from -6 to 6
- conditioning: bfloat16 [16, 768], P('dp'), may hold values from -6 to 6
- live_counts: int32 [8], P('dp'), may hold values from 1 to 2, as said below
- ada_weight: bfloat16 [768, 4608], P(None, 'tensor'), may hold values from -0.21875 to 0.21875
- ada_bias: float32 [4608], P('tensor'), may hold values from -3 to 3
- qkv_weight: bfloat16 [768, 3, 768], P(None, None, 'tensor'), may hold values from -4 to 4, as said below
- qv_bias: float32 [2, 768], P(None, 'tensor'), may hold values from -3 to 3
- proj_weight: bfloat16 [768, 768], P('tensor'), may hold values from -0.875 to 0.875
- proj_bias: float32 [768], replicated, may hold values from -3 to 3
- dense1_weight: bfloat16 [768, 3072], P(None, 'tensor'), may hold values from -0.21875 to 0.21875
- dense1_bias: float32 [3072], P('tensor'), may hold values from -3 to 3
- dense2_weight: bfloat16 [3072, 768], P('tensor'), may hold values from -0.109375 to 0.109375
- dense2_bias: float32 [768], replicated, may hold values from -3 to 3
- cotangent: bfloat16 [16, 256, 768], P('dp'), may hold values from -6 to 6
Outputs:
- block_output: bfloat16 [16, 256, 768], P('dp')
- grad_latents: float32 [16, 256, 768], P('dp')
- grad_conditioning: float32 [16, 768], P('dp')
- grad_ada_weight: float32 [768, 4608], P('dp', 'tensor')
- grad_ada_bias: float32 [4608], P('tensor')
- grad_qkv_weight: float32 [768, 3, 768], P('dp', None, 'tensor')
- grad_qv_bias: float32 [2, 768], P(None, 'tensor')
- grad_proj_weight: float32 [768, 768], P('tensor', 'dp')
- grad_proj_bias: float32 [768], replicated
- grad_fc1_weight: float32 [768, 3072], P('dp', 'tensor')
- grad_fc1_bias: float32 [3072], P('tensor')
- grad_fc2_weight: float32 [3072, 768], P('tensor', 'dp')
- grad_fc2_bias: float32 [768], replicated
The draws below stay inside these ranges and needn't reach their ends.
Inputs may be any that keep to these rules, and one draw needn't show every extreme that they name: `live_counts`: each entry counts the live latents of one dp index; they fill its first slots. Some index holds 2, some holds 1. `qkv_weight`: entries are of order D ** -0.5.
All inputs are finite; a program needn't handle non-finite values.
Results may differ from the reference program's by a relative error of at most 0.012.
The reference program's roundings to bfloat16 on the way count: a program that leaves them out, or rounds other values in their place, can miss the bound.
Values may be sent and summed in bfloat16 or wider, within the bound.
A program may use at most 128 MiB of HBM per device.

```python
import math
import jax
import jax.numpy as jnp
from jax import lax

D = 768
FF = 3072
H = 12
HD = 64
SEQ = 256
LAT_CAP = 2
LATENTS = 16
N_DP = 8


def draw_live_counts(key, part):
    roll = jax.random.randint(jax.random.fold_in(key, 21), (N_DP,), 0, 8)
    counts = jnp.where(roll < 1, LAT_CAP, jnp.where(roll < 3, (LAT_CAP + 1) // 2, 1))
    first_pick = jax.random.randint(jax.random.fold_in(key, 22), (), 0, N_DP)
    offset = jax.random.randint(jax.random.fold_in(key, 23), (), 1, N_DP)
    second_pick = (first_pick + offset) % N_DP
    positions = jnp.arange(N_DP)
    counts = jnp.where(positions == first_pick, LAT_CAP, counts)
    counts = jnp.where(positions == second_pick, 1, counts)
    return counts.astype(jnp.int32)


def draw_qkv_weight(key, part):
    key_main = jax.random.fold_in(key, 31)
    base = jnp.clip(jax.random.normal(key_main, (D, 3, D), jnp.float32), -4.0, 4.0)
    weights = base * D ** (-0.5)
    return weights.astype(jnp.bfloat16)


def raised(entries, own_key, source, target, blocks, factor):
    def block_of(dim):
        return (jnp.arange(entries.shape[dim]) // (entries.shape[dim] // blocks)).reshape((-1,) + (1,) * (entries.ndim - 1 - dim))

    near = jax.random.permutation(own_key, blocks)[block_of(target)]
    far = (block_of(target) + blocks // 2) % blocks
    return jnp.where((block_of(source) == near) | (block_of(source) == far), factor * entries, entries)


def block_levels(key, shape, shards, least, top_value):
    factor_of = 1.0
    for axis_at, blocks in shards:
        draws = jax.random.uniform(jax.random.fold_in(jax.random.fold_in(key, 6), axis_at), (blocks,), jnp.float32, least / len(shards), top_value / len(shards))
        factor_of = factor_of * jnp.repeat(jnp.exp(draws), shape[axis_at] // blocks).reshape((-1,) + (1,) * (len(shape) - 1 - axis_at))
    return factor_of


def bell_draw(stream_key, extent, spread, most, cuts=(), kind=jnp.bfloat16):
    level = block_levels(stream_key, extent, cuts, -0.22, 0.18) if cuts else 1.0
    array = jax.random.normal(stream_key, extent, jnp.float32) * spread * level
    return jnp.minimum(jnp.maximum(array, -most), most).astype(kind)


def noise_with(stream_key, dims, scale, reach, cuts, heavy, held_as=jnp.bfloat16):
    values = scale * jax.random.normal(stream_key, dims, jnp.float32)
    if cuts:
        values = values * block_levels(stream_key, dims, cuts, -0.22, 0.18)
    return jnp.clip(raised(values, jax.random.fold_in(stream_key, 3), *heavy), -reach, reach).astype(held_as)


def setup_inputs(seed: int = 0) -> dict:
    key_of = jax.random.split(jax.random.key(seed), 15)
    latents = bell_draw(key_of[0], (LATENTS, SEQ, D), 1.0, 6.0, ((0, 8),))
    conditioning = bell_draw(key_of[1], (LATENTS, D), 1.0, 6.0, ((0, 8),))
    live_counts = draw_live_counts(jax.random.fold_in(key_of[14], 71), 0)
    ada_weight = bell_draw(key_of[3], (D, 6 * D), D ** -0.5, 0.21875, ((1, 4),))
    ada_bias = bell_draw(key_of[4], (6 * D,), 0.5, 3.0, ((0, 4),), jnp.float32)
    qkv_weight = draw_qkv_weight(jax.random.fold_in(key_of[14], 71), 0)
    qv_bias = bell_draw(key_of[6], (2, D), 0.5, 3.0, ((1, 4),), jnp.float32)
    proj_weight = bell_draw(key_of[7], (D, D), (D // 16) ** -0.5, 0.875, ((0, 4),))
    proj_bias = bell_draw(key_of[8], (D,), 0.5, 3.0, (), jnp.float32)
    dense1_weight = bell_draw(key_of[9], (D, FF), D ** -0.5, 0.21875, ((1, 4),))
    dense1_bias = bell_draw(key_of[10], (FF,), 0.5, 3.0, ((0, 4),), jnp.float32)
    dense2_weight = bell_draw(key_of[11], (FF, D), FF ** -0.5, 0.109375, ((0, 4),))
    dense2_bias = bell_draw(key_of[12], (D,), 0.5, 3.0, (), jnp.float32)
    cotangent = noise_with(key_of[13], (LATENTS, SEQ, D), 1.0, 6.0, ((0, 8),), (0, 2, 8, 2.0))
    return dict(latents=latents, conditioning=conditioning, live_counts=live_counts, ada_weight=ada_weight, ada_bias=ada_bias, qkv_weight=qkv_weight, qv_bias=qv_bias, proj_weight=proj_weight, proj_bias=proj_bias, dense1_weight=dense1_weight, dense1_bias=dense1_bias, dense2_weight=dense2_weight, dense2_bias=dense2_bias, cotangent=cotangent)


EPS = 1e-06
GELU_C = math.sqrt(2.0 / math.pi)

def contract_exact(form, left, right):
    return jnp.einsum(form, left.astype(jnp.float32), right.astype(jnp.float32), precision=lax.Precision.HIGHEST)

def silu_slope(values):
    sig = jax.nn.sigmoid(values)
    return sig * (1.0 + values * (1.0 - sig))

def gelu_slope(values):
    tangent = jnp.tanh(GELU_C * (values + 0.044715 * values * values * values))
    return 0.5 * (1.0 + tangent) + 0.5 * values * (1.0 - tangent * tangent) * GELU_C * (1.0 + 3.0 * 0.044715 * values * values)

def norm_rows(values):
    center = values - lax.optimization_barrier(jnp.mean(values, axis=-1, keepdims=True))
    recip = lax.rsqrt(lax.optimization_barrier(jnp.mean(center * center, axis=-1, keepdims=True)) + EPS)
    return (center * recip, recip)

def norm_back(grad_norm, normed, recip):
    return recip * (grad_norm - lax.optimization_barrier(jnp.mean(grad_norm, axis=-1, keepdims=True)) - normed * lax.optimization_barrier(jnp.mean(grad_norm * normed, axis=-1, keepdims=True)))

def block_pass(tokens, cond_rows, live_rows, cot_rows, ada_weight, ada_bias, qkv_weight, qv_bias, proj_weight, proj_bias, dense1_weight, dense1_bias, dense2_weight, dense2_bias):
    lat_num = tokens.shape[0]
    cond_f = cond_rows.astype(jnp.float32)
    silu_b = jax.nn.silu(cond_f).astype(jnp.bfloat16)
    modulation = contract_exact('ld,de->le', silu_b, ada_weight) + ada_bias
    blocks = modulation.reshape(lat_num, 6, D)[:, :, None, :]
    shift_one, scale_one, gate_one = (blocks[:, 0], blocks[:, 1], blocks[:, 2])
    shift_two, scale_two, gate_two = (blocks[:, 3], blocks[:, 4], blocks[:, 5])
    tokens_f = tokens.astype(jnp.float32)
    norm_one, recip_one = norm_rows(tokens_f)
    h_one = (norm_one * (1.0 + scale_one) + shift_one).astype(jnp.bfloat16)
    qkv_rows = contract_exact('lsd,dce->lsce', h_one, qkv_weight)
    queries = (qkv_rows[:, :, 0] + qv_bias[0]).astype(jnp.bfloat16).reshape(lat_num, SEQ, H, HD)
    key_rows = qkv_rows[:, :, 1].astype(jnp.bfloat16).reshape(lat_num, SEQ, H, HD)
    value_rows = (qkv_rows[:, :, 2] + qv_bias[1]).astype(jnp.bfloat16).reshape(lat_num, SEQ, H, HD)
    scale_qk = HD ** (-0.5)
    scores = contract_exact('lqhe,lkhe->lhqk', queries, key_rows) * scale_qk
    log_total = jax.nn.logsumexp(scores, axis=-1, keepdims=True)
    probs_b = jnp.exp(scores - log_total).astype(jnp.bfloat16)
    attended = contract_exact('lhqk,lkhe->lqhe', probs_b, value_rows).astype(jnp.bfloat16).reshape(lat_num, SEQ, D)
    attn_branch = contract_exact('lsd,de->lse', attended, proj_weight) + proj_bias
    x_one = tokens_f + gate_one * attn_branch
    norm_two, recip_two = norm_rows(x_one)
    hidden_second = (norm_two * (1.0 + scale_two) + shift_two).astype(jnp.bfloat16)
    preactivation_rows = contract_exact('kow,wz->koz', hidden_second, dense1_weight) + dense1_bias
    activation_lowprec = jax.nn.gelu(preactivation_rows, approximate=True).astype(jnp.bfloat16)
    perceptron_branch = contract_exact('jqv,vg->jqg', activation_lowprec, dense2_weight) + dense2_bias
    live_f = live_rows[:, None, None]
    block_output = (live_f * (x_one + gate_two * perceptron_branch)).astype(jnp.bfloat16)
    grad_out = live_f * cot_rows.astype(jnp.float32)
    dgate_two = lax.optimization_barrier(jnp.sum(grad_out * perceptron_branch, axis=1))
    dmlp = gate_two * grad_out
    perceptron_gradient_lowprec = dmlp.astype(jnp.bfloat16)
    dense2_gradient = contract_exact('kby,kbi->yi', activation_lowprec, perceptron_gradient_lowprec)
    grad_fc2_b = lax.optimization_barrier(jnp.sum(dmlp, axis=(0, 1)))
    activation_gradient = contract_exact('vug,bg->vub', perceptron_gradient_lowprec, dense2_weight)
    dpre = activation_gradient * gelu_slope(preactivation_rows)
    preactivation_gradient_lowprec = dpre.astype(jnp.bfloat16)
    dense1_gradient = contract_exact('qmw,qmx->wx', hidden_second, preactivation_gradient_lowprec)
    grad_fc1_b = lax.optimization_barrier(jnp.sum(dpre, axis=(0, 1)))
    hidden_second_gradient = contract_exact('hnb,jb->hnj', preactivation_gradient_lowprec, dense1_weight)
    dscale_two = lax.optimization_barrier(jnp.sum(hidden_second_gradient * norm_two, axis=1))
    dshift_two = lax.optimization_barrier(jnp.sum(hidden_second_gradient, axis=1))
    dx_one = grad_out + norm_back(hidden_second_gradient * (1.0 + scale_two), norm_two, recip_two)
    dattn = gate_one * dx_one
    dgate_one = lax.optimization_barrier(jnp.sum(dx_one * attn_branch, axis=1))
    dattn_b = dattn.astype(jnp.bfloat16)
    grad_proj = contract_exact('lsd,lse->de', attended, dattn_b)
    grad_proj_b = lax.optimization_barrier(jnp.sum(dattn, axis=(0, 1)))
    dattended = contract_exact('lse,de->lsd', dattn_b, proj_weight).astype(jnp.bfloat16).reshape(lat_num, SEQ, H, HD)
    scores_again = contract_exact('lqhe,lkhe->lhqk', queries, key_rows) * scale_qk
    probs = jnp.exp(scores_again - log_total)
    probs_again = probs.astype(jnp.bfloat16)
    dprobs = contract_exact('lqhe,lkhe->lhqk', dattended, value_rows)
    delta = lax.optimization_barrier(jnp.sum(probs * dprobs, axis=-1, keepdims=True))
    dscores_b = (probs * (dprobs - delta) * scale_qk).astype(jnp.bfloat16)
    dquery = contract_exact('lhqk,lkhe->lqhe', dscores_b, key_rows).reshape(lat_num, SEQ, D)
    dkey = contract_exact('lhqk,lqhe->lkhe', dscores_b, queries).reshape(lat_num, SEQ, D)
    dvalue = contract_exact('lhqk,lqhe->lkhe', probs_again, dattended).reshape(lat_num, SEQ, D)
    grad_qv = jnp.stack([lax.optimization_barrier(jnp.sum(dquery, axis=(0, 1))), lax.optimization_barrier(jnp.sum(dvalue, axis=(0, 1)))], axis=0)
    dqkv_b = jnp.stack([dquery, dkey, dvalue], axis=2).astype(jnp.bfloat16)
    grad_qkv = contract_exact('lsd,lsce->dce', h_one, dqkv_b)
    dh_one = contract_exact('lsce,dce->lsd', dqkv_b, qkv_weight)
    dscale_one = lax.optimization_barrier(jnp.sum(dh_one * norm_one, axis=1))
    dshift_one = lax.optimization_barrier(jnp.sum(dh_one, axis=1))
    grad_tokens = dx_one + norm_back(dh_one * (1.0 + scale_one), norm_one, recip_one)
    dmod = jnp.stack([dshift_one, dscale_one, dgate_one, dshift_two, dscale_two, dgate_two], axis=1).reshape(lat_num, 6 * D)
    dmod_b = dmod.astype(jnp.bfloat16)
    grad_ada = contract_exact('ld,le->de', silu_b, dmod_b)
    grad_ada_b = lax.optimization_barrier(jnp.sum(dmod, axis=0))
    grad_cond = contract_exact('le,de->ld', dmod_b, ada_weight) * silu_slope(cond_f)
    grads = (grad_ada, grad_ada_b, grad_qkv, grad_qv, grad_proj, grad_proj_b, dense1_gradient, grad_fc1_b, dense2_gradient, grad_fc2_b)
    return (block_output, grad_tokens, grad_cond, grads)

def reference(latents, conditioning, live_counts, ada_weight, ada_bias, qkv_weight, qv_bias, proj_weight, proj_bias, dense1_weight, dense1_bias, dense2_weight, dense2_bias, cotangent):
    live = (jnp.arange(LAT_CAP, dtype=jnp.int32)[None, :] < live_counts[:, None]).astype(jnp.float32)
    token_blocks = latents.reshape(N_DP, LAT_CAP, SEQ, D)
    cond_blocks = conditioning.reshape(N_DP, LAT_CAP, D)
    cot_blocks = cotangent.reshape(N_DP, LAT_CAP, SEQ, D)
    initial = (jnp.zeros((D, 6 * D), jnp.float32), jnp.zeros((6 * D,), jnp.float32), jnp.zeros((D, 3, D), jnp.float32), jnp.zeros((2, D), jnp.float32), jnp.zeros((D, D), jnp.float32), jnp.zeros((D,), jnp.float32), jnp.zeros((D, FF), jnp.float32), jnp.zeros((FF,), jnp.float32), jnp.zeros((FF, D), jnp.float32), jnp.zeros((D,), jnp.float32))

    def step_fn(totals, pieces):
        tokens, cond_rows, live_rows, cot_rows = pieces
        block_output, grad_tokens, grad_cond, grads = block_pass(tokens, cond_rows, live_rows, cot_rows, ada_weight, ada_bias, qkv_weight, qv_bias, proj_weight, proj_bias, dense1_weight, dense1_bias, dense2_weight, dense2_bias)
        totals = tuple((total + piece for total, piece in zip(totals, grads)))
        return (totals, (block_output, grad_tokens, grad_cond))
    totals, stacked = lax.scan(step_fn, initial, (token_blocks, cond_blocks, live, cot_blocks))
    block_output = stacked[0].reshape(LATENTS, SEQ, D)
    grad_latents = stacked[1].reshape(LATENTS, SEQ, D)
    grad_conditioning = stacked[2].reshape(LATENTS, D)
    return (block_output, grad_latents, grad_conditioning, totals[0], totals[1], totals[2], totals[3], totals[4], totals[5], totals[6], totals[7], totals[8], totals[9])
```

```python
import functools
import math

import jax
import jax.numpy as jnp
from jax import lax
from jax.experimental import pallas as pl
from jax.experimental.pallas import tpu as pltpu
from jax.sharding import PartitionSpec as P

HD = 64


EPS = 1e-06
GELU_C = math.sqrt(2.0 / math.pi)


def to_half(values):
    return values.astype(jnp.bfloat16)


def silu_slope(values):
    sig = jax.nn.sigmoid(values)
    return sig * (1.0 + values * (1.0 - sig))


def gelu_slope(values):
    tangent = jnp.tanh(GELU_C * (values + 0.044715 * values * values * values))
    return 0.5 * (1.0 + tangent) + 0.5 * values * (1.0 - tangent * tangent) * GELU_C * (
        1.0 + 3.0 * 0.044715 * values * values
    )


def norm_rows(values):
    center = values - jnp.mean(values, axis=-1, keepdims=True)
    recip = lax.rsqrt(jnp.mean(center * center, axis=-1, keepdims=True) + EPS)
    return (center * recip, recip)


def norm_back(grad_norm, normed, recip):
    return recip * (
        grad_norm
        - jnp.mean(grad_norm, axis=-1, keepdims=True)
        - normed * jnp.mean(grad_norm * normed, axis=-1, keepdims=True)
    )


def contract_lowprec(form, left, right):
    return jnp.einsum(form, left, right, preferred_element_type=jnp.float32)


def exchange_body(kinds, sizes, copy_count, *refs):
    count = len(kinds)
    ins, outs = refs[:count], refs[count : 2 * count]
    send_sem, recv_sem, local_sem = refs[2 * count :]
    axes = [axis for axis in ("tensor", "dp") if any(k[0] == axis for k in kinds)]
    me = {axis: lax.axis_index(axis) for axis in axes}
    barrier = pltpu.get_barrier_semaphore()
    peers = 0
    for axis in axes:
        for step in range(1, sizes[axis]):
            pl.semaphore_signal(
                barrier,
                inc=1,
                device_id={axis: lax.rem(me[axis] + step, sizes[axis])},
                device_id_type=pl.DeviceIdType.MESH,
            )
            peers += 1
    pl.semaphore_wait(barrier, peers)
    started = []
    slot = 0
    for step in range(1, max(sizes.values())):
        for (axis, form), src, dst in zip(kinds, ins, outs):
            size = sizes[axis]
            if step >= size:
                continue
            target = lax.rem(me[axis] + step, size)
            if form == "gather_rows":
                rows = src.shape[1]
                source = src
                place = dst.at[:, pl.ds(pl.multiple_of(me[axis] * rows, rows), rows)]
            elif form == "gather":
                source, place = src, dst.at[me[axis]]
            elif form == "scatter_rows":
                rows = src.shape[1] // size
                source = src.at[:, pl.ds(pl.multiple_of(target * rows, rows), rows)]
                place = dst.at[step - 1]
            else:
                source, place = src.at[target], dst.at[step - 1]
            copy = pltpu.make_async_remote_copy(
                src_ref=source,
                dst_ref=place,
                send_sem=send_sem.at[slot],
                recv_sem=recv_sem.at[slot],
                device_id={axis: target},
                device_id_type=pl.DeviceIdType.MESH,
            )
            copy.start()
            started.append(copy)
            slot += 1
    for index, ((axis, form), src, dst) in enumerate(zip(kinds, ins, outs)):
        if form == "gather_rows":
            rows = src.shape[1]
            place = dst.at[:, pl.ds(pl.multiple_of(me[axis] * rows, rows), rows)]
        elif form == "gather":
            place = dst.at[me[axis]]
        else:
            continue
        copy = pltpu.make_async_copy(src, place, local_sem.at[index])
        copy.start()
        started.append(copy)
    for copy in started:
        copy.wait()


def exchange(ident, *items):
    sizes = {"tensor": lax.axis_size("tensor"), "dp": lax.axis_size("dp")}
    kinds = tuple((axis, form) for axis, form, _ in items)
    shapes = []
    for axis, form, array in items:
        size = sizes[axis]
        if form == "gather_rows":
            shape = (array.shape[0], array.shape[1] * size, array.shape[2])
        elif form == "gather":
            shape = (size,) + array.shape
        elif form == "scatter_rows":
            shape = (size - 1, array.shape[0], array.shape[1] // size, array.shape[2])
        else:
            shape = (size - 1,) + array.shape[1:]
        shapes.append(jax.ShapeDtypeStruct(shape, array.dtype))
    copy_count = sum(sizes[axis] - 1 for axis, _ in kinds)
    return pl.pallas_call(
        functools.partial(exchange_body, kinds, sizes, copy_count),
        out_shape=shapes,
        in_specs=[pl.BlockSpec(memory_space=pl.ANY)] * len(items),
        out_specs=[pl.BlockSpec(memory_space=pl.ANY)] * len(items),
        scratch_shapes=[
            pltpu.SemaphoreType.DMA((copy_count,)),
            pltpu.SemaphoreType.DMA((copy_count,)),
            pltpu.SemaphoreType.DMA((len(items),)),
        ],
        compiler_params=pltpu.CompilerParams(collective_id=ident, has_side_effects=True),
    )(*[array for _, _, array in items])


def sum_rows(piece, arrived, start):
    own = lax.dynamic_slice_in_dim(piece, start, arrived.shape[2], 1).astype(jnp.float32)
    return own + jnp.sum(arrived.astype(jnp.float32), axis=0)


def sum_blocks(pieces, arrived, index):
    own = lax.dynamic_index_in_dim(pieces, index, 0, keepdims=False).astype(jnp.float32)
    return own + jnp.sum(arrived.astype(jnp.float32), axis=0)


def per_device(
    latents,
    conditioning,
    live_counts,
    ada_weight,
    ada_bias,
    qkv_weight,
    qv_bias,
    proj_weight,
    proj_bias,
    dense1_weight,
    dense1_bias,
    dense2_weight,
    dense2_bias,
    cotangent,
):
    lat_cap, seq_len, width = latents.shape
    head_count = qkv_weight.shape[2] // HD
    local_width = head_count * HD
    local_cols = ada_weight.shape[1]
    local_hidden = dense1_weight.shape[1]
    tensor_count = lax.axis_size("tensor")
    tensor_index = lax.axis_index("tensor")
    dp_count = lax.axis_size("dp")
    dp_index = lax.axis_index("dp")
    rows_dev = seq_len // tensor_count
    row_start = tensor_index * rows_dev
    scale_qk = HD ** (-0.5)
    live_mask = (jnp.arange(lat_cap) < live_counts[0]).astype(jnp.float32)[:, None, None]
    cond_f = conditioning.astype(jnp.float32)
    silu_b = to_half(jax.nn.silu(cond_f))
    mod_part = jnp.dot(silu_b, ada_weight, preferred_element_type=jnp.float32) + ada_bias
    mod_all, silu_all = exchange(
        1, ("tensor", "gather", mod_part), ("dp", "gather", silu_b.astype(jnp.float32))
    )
    modulation = jnp.swapaxes(mod_all, 0, 1).reshape(lat_cap, 6 * width)
    blocks = modulation.reshape(lat_cap, 6, width)[:, :, None, :]
    shift_one, scale_one, gate_one = (blocks[:, 0], blocks[:, 1], blocks[:, 2])
    shift_two, scale_two, gate_two = (blocks[:, 3], blocks[:, 4], blocks[:, 5])
    tokens_f = latents.astype(jnp.float32)
    norm_one, recip_one = norm_rows(tokens_f)
    h_one = to_half(norm_one * (1.0 + scale_one) + shift_one)
    qkv_rows = contract_lowprec("lsd,dce->lsce", h_one, qkv_weight)
    queries = to_half(qkv_rows[:, :, 0] + qv_bias[0]).reshape(lat_cap, seq_len, head_count, HD)
    key_rows = to_half(qkv_rows[:, :, 1]).reshape(lat_cap, seq_len, head_count, HD)
    value_rows = to_half(qkv_rows[:, :, 2] + qv_bias[1]).reshape(lat_cap, seq_len, head_count, HD)
    scores = contract_lowprec("lqhe,lkhe->lhqk", queries, key_rows) * scale_qk
    log_total = jax.nn.logsumexp(scores, axis=-1, keepdims=True)
    probs_b = to_half(jnp.exp(scores - log_total))
    attended = to_half(contract_lowprec("lhqk,lkhe->lqhe", probs_b, value_rows)).reshape(
        lat_cap, seq_len, local_width
    )
    attn_part = to_half(contract_lowprec("lsd,de->lse", attended, proj_weight))
    (attn_arrived,) = exchange(2, ("tensor", "scatter_rows", attn_part))
    attn_branch = sum_rows(attn_part, attn_arrived, row_start) + proj_bias
    tokens_own = lax.dynamic_slice_in_dim(tokens_f, row_start, rows_dev, 1)
    x_one = tokens_own + gate_one * attn_branch
    norm_two, recip_two = norm_rows(x_one)
    hidden_own = to_half(norm_two * (1.0 + scale_two) + shift_two)
    (hidden_second,) = exchange(3, ("tensor", "gather_rows", hidden_own))
    preactivation_rows = contract_lowprec("kow,wz->koz", hidden_second, dense1_weight) + dense1_bias
    activation_lowprec = to_half(jax.nn.gelu(preactivation_rows, approximate=True))
    perceptron_piece = to_half(contract_lowprec("jqv,vg->jqg", activation_lowprec, dense2_weight))
    dmlp = gate_two * (live_mask * cotangent.astype(jnp.float32))
    perceptron_gradient_lowprec = to_half(dmlp)
    grad_fc2_part = jnp.sum(dmlp, axis=(0, 1))
    dense2_gradient = to_half(
        contract_lowprec("kbi,kby->iy", perceptron_gradient_lowprec, activation_lowprec)
    ).reshape(dp_count, width // dp_count, local_hidden)
    activation_gradient = contract_lowprec(
        "vug,bg->vub", perceptron_gradient_lowprec, dense2_weight
    )
    dpre = activation_gradient * gelu_slope(preactivation_rows)
    preactivation_gradient_lowprec = to_half(dpre)
    dense1_gradient = to_half(
        contract_lowprec("qmw,qmx->wx", hidden_second, preactivation_gradient_lowprec)
    ).reshape(dp_count, width // dp_count, local_hidden)
    grad_fc1_b = jnp.sum(dpre, axis=(0, 1))
    hidden_gradient_piece = to_half(
        contract_lowprec("hnb,jb->hnj", preactivation_gradient_lowprec, dense1_weight)
    )
    hidden_arrived, perceptron_arrived, fc1_arrived, fc2_arrived = exchange(
        4,
        ("tensor", "scatter_rows", hidden_gradient_piece),
        ("tensor", "scatter_rows", perceptron_piece),
        ("dp", "scatter", dense1_gradient),
        ("dp", "scatter", dense2_gradient),
    )
    summed_fc1 = sum_blocks(dense1_gradient, fc1_arrived, dp_index)
    summed_fc2 = sum_blocks(dense2_gradient, fc2_arrived, dp_index).T
    hidden_second_gradient = sum_rows(hidden_gradient_piece, hidden_arrived, row_start)
    perceptron_branch = sum_rows(perceptron_piece, perceptron_arrived, row_start) + dense2_bias
    output_own = to_half(live_mask * (x_one + gate_two * perceptron_branch))
    cot_own = lax.dynamic_slice_in_dim(cotangent, row_start, rows_dev, 1)
    grad_out = live_mask * cot_own.astype(jnp.float32)
    dgate_two = jnp.sum(grad_out * perceptron_branch, axis=1)
    dscale_two = jnp.sum(hidden_second_gradient * norm_two, axis=1)
    dshift_two = jnp.sum(hidden_second_gradient, axis=1)
    dx_one = grad_out + norm_back(hidden_second_gradient * (1.0 + scale_two), norm_two, recip_two)
    dattn = gate_one * dx_one
    dgate_one = jnp.sum(dx_one * attn_branch, axis=1)
    dattn_own_b = to_half(dattn)
    grad_proj_part = jnp.sum(dattn, axis=(0, 1))
    dattn_b, block_output = exchange(
        5, ("tensor", "gather_rows", dattn_own_b), ("tensor", "gather_rows", output_own)
    )
    grad_proj = contract_lowprec("lse,lsd->ed", dattn_b, attended)
    dattended = to_half(contract_lowprec("lse,de->lsd", dattn_b, proj_weight)).reshape(
        lat_cap, seq_len, head_count, HD
    )
    scores_again = contract_lowprec("lqhe,lkhe->lhqk", queries, key_rows) * scale_qk
    probs = jnp.exp(scores_again - log_total)
    probs_again = to_half(probs)
    dprobs = contract_lowprec("lqhe,lkhe->lhqk", dattended, value_rows)
    delta = jnp.sum(probs * dprobs, axis=-1, keepdims=True)
    dscores_b = to_half(probs * (dprobs - delta) * scale_qk)
    dquery = contract_lowprec("lhqk,lkhe->lqhe", dscores_b, key_rows).reshape(
        lat_cap, seq_len, local_width
    )
    dkey = contract_lowprec("lhqk,lqhe->lkhe", dscores_b, queries).reshape(
        lat_cap, seq_len, local_width
    )
    dvalue = contract_lowprec("lhqk,lqhe->lkhe", probs_again, dattended).reshape(
        lat_cap, seq_len, local_width
    )
    grad_qv = jnp.stack([jnp.sum(dquery, axis=(0, 1)), jnp.sum(dvalue, axis=(0, 1))], axis=0)
    dqkv_b = to_half(jnp.stack([dquery, dkey, dvalue], axis=2))
    grad_qkv = contract_lowprec("lsd,lsce->dce", h_one, dqkv_b)
    dh_part_one = to_half(contract_lowprec("lsce,dce->lsd", dqkv_b, qkv_weight))
    attn_gradient = jnp.concatenate(
        [to_half(grad_qkv).reshape(width, 3 * local_width), to_half(grad_proj)], axis=1
    ).reshape(dp_count, width // dp_count, 4 * local_width)
    dh_arrived, attn_gradient_arrived = exchange(
        6, ("tensor", "scatter_rows", dh_part_one), ("dp", "scatter", attn_gradient)
    )
    summed_attn = sum_blocks(attn_gradient, attn_gradient_arrived, dp_index)
    summed_qkv = summed_attn[:, : 3 * local_width].reshape(-1, 3, local_width)
    summed_proj = summed_attn[:, 3 * local_width :].T
    dh_one = sum_rows(dh_part_one, dh_arrived, row_start)
    norm_one_own = lax.dynamic_slice_in_dim(norm_one, row_start, rows_dev, 1)
    recip_one_own = lax.dynamic_slice_in_dim(recip_one, row_start, rows_dev, 1)
    dscale_one = jnp.sum(dh_one * norm_one_own, axis=1)
    dshift_one = jnp.sum(dh_one, axis=1)
    grad_own = dx_one + norm_back(dh_one * (1.0 + scale_one), norm_one_own, recip_one_own)
    stats_own = jnp.concatenate(
        [
            jnp.stack(
                [dshift_one, dscale_one, dgate_one, dshift_two, dscale_two, dgate_two], axis=1
            ).reshape(lat_cap * 6, width),
            grad_proj_part[None],
        ],
        axis=0,
    )
    grad_gathered, stats_all = exchange(
        7, ("tensor", "gather_rows", to_half(grad_own)), ("tensor", "gather", stats_own)
    )
    grad_latents = grad_gathered.astype(jnp.float32)
    stats_sum = jnp.sum(stats_all, axis=0)
    dmod = stats_sum[: lat_cap * 6].reshape(lat_cap, 6 * width)
    col_start = tensor_index * local_cols
    dmod_local = lax.dynamic_slice_in_dim(dmod, col_start, local_cols, 1)
    cond_part = contract_lowprec("le,de->ld", to_half(dmod_local), ada_weight)
    parts = [
        dmod_local.reshape(-1),
        grad_qv.reshape(-1),
        grad_fc1_b,
        grad_fc2_part,
        stats_sum[lat_cap * 6],
    ]
    packed_all, cond_all = exchange(
        8, ("dp", "gather", jnp.concatenate(parts)[None]), ("tensor", "gather", cond_part)
    )
    grad_conditioning = jnp.sum(cond_all, axis=0) * silu_slope(cond_f)
    packed_all = packed_all[:, 0]
    dmod_cols = lat_cap * local_cols
    dmod_all = packed_all[:, :dmod_cols].reshape(dp_count * lat_cap, local_cols)
    bias_ada = jnp.sum(dmod_all, axis=0)
    block = width // dp_count
    silu_own = lax.dynamic_slice_in_dim(
        to_half(silu_all).reshape(dp_count * lat_cap, width), dp_index * block, block, 1
    )
    summed_ada = contract_lowprec("ld,le->de", silu_own, to_half(dmod_all))
    totals = jnp.sum(packed_all[:, dmod_cols:], axis=0)
    bias_qv, bias_fc1, fc2_tot, proj_tot = jnp.split(
        totals,
        (2 * local_width, 2 * local_width + local_hidden, 2 * local_width + local_hidden + width),
    )
    bias_qv = bias_qv.reshape(2, local_width)
    return (
        block_output,
        grad_latents,
        grad_conditioning,
        summed_ada,
        bias_ada,
        summed_qkv,
        bias_qv,
        summed_proj,
        proj_tot,
        summed_fc1,
        bias_fc1,
        summed_fc2,
        fc2_tot,
    )


def solution(mesh):
    placed = (
        P("dp", None, None),
        P("dp", None),
        P("dp"),
        P(None, "tensor"),
        P("tensor"),
        P(None, None, "tensor"),
        P(None, "tensor"),
        P("tensor", None),
        P(),
        P(None, "tensor"),
        P("tensor"),
        P("tensor", None),
        P(),
        P("dp", None, None),
    )
    return jax.shard_map(
        per_device,
        mesh=mesh,
        in_specs=placed,
        out_specs=(
            P("dp", None, None),
            P("dp", None, None),
            P("dp", None),
            P("dp", "tensor"),
            P("tensor"),
            P("dp", None, "tensor"),
            P(None, "tensor"),
            P("tensor", "dp"),
            P(),
            P("dp", "tensor"),
            P("tensor"),
            P("tensor", "dp"),
            P(),
        ),
        check_vma=False,
    )
```

```python
import functools
import math

import jax
import jax.numpy as jnp
from jax import lax
from jax.experimental import pallas as pl
from jax.experimental.pallas import tpu as pltpu
from jax.sharding import PartitionSpec as P

HD = 64


EPS = 1e-06
GELU_C = math.sqrt(2.0 / math.pi)


def to_half(values):
    return values.astype(jnp.bfloat16)


def silu_slope(values):
    sig = jax.nn.sigmoid(values)
    return sig * (1.0 + values * (1.0 - sig))


def gelu_slope(values):
    tangent = jnp.tanh(GELU_C * (values + 0.044715 * values * values * values))
    return 0.5 * (1.0 + tangent) + 0.5 * values * (1.0 - tangent * tangent) * GELU_C * (
        1.0 + 3.0 * 0.044715 * values * values
    )


def norm_rows(values):
    center = values - jnp.mean(values, axis=-1, keepdims=True)
    recip = lax.rsqrt(jnp.mean(center * center, axis=-1, keepdims=True) + EPS)
    return (center * recip, recip)


def norm_back(grad_norm, normed, recip):
    return recip * (
        grad_norm
        - jnp.mean(grad_norm, axis=-1, keepdims=True)
        - normed * jnp.mean(grad_norm * normed, axis=-1, keepdims=True)
    )


def contract_lowprec(form, left, right):
    return jnp.einsum(form, left, right, preferred_element_type=jnp.float32)


def exchange_body(kinds, sizes, copy_count, *refs):
    count = len(kinds)
    ins, outs = refs[:count], refs[count : 2 * count]
    send_sem, recv_sem, local_sem = refs[2 * count :]
    axes = [axis for axis in ("tensor", "dp") if any(k[0] == axis for k in kinds)]
    me = {axis: lax.axis_index(axis) for axis in axes}
    barrier = pltpu.get_barrier_semaphore()
    peers = 0
    for axis in axes:
        for step in range(1, sizes[axis]):
            pl.semaphore_signal(
                barrier,
                inc=1,
                device_id={axis: lax.rem(me[axis] + step, sizes[axis])},
                device_id_type=pl.DeviceIdType.MESH,
            )
            peers += 1
    pl.semaphore_wait(barrier, peers)
    started = []
    slot = 0
    for step in range(1, max(sizes.values())):
        for (axis, form), src, dst in zip(kinds, ins, outs):
            size = sizes[axis]
            if step >= size:
                continue
            target = lax.rem(me[axis] + step, size)
            if form == "gather_rows":
                rows = src.shape[1]
                source = src
                place = dst.at[:, pl.ds(pl.multiple_of(me[axis] * rows, rows), rows)]
            elif form == "gather":
                source, place = src, dst.at[me[axis]]
            elif form == "scatter_rows":
                rows = src.shape[1] // size
                source = src.at[:, pl.ds(pl.multiple_of(target * rows, rows), rows)]
                place = dst.at[step - 1]
            else:
                source, place = src.at[target], dst.at[step - 1]
            copy = pltpu.make_async_remote_copy(
                src_ref=source,
                dst_ref=place,
                send_sem=send_sem.at[slot],
                recv_sem=recv_sem.at[slot],
                device_id={axis: target},
                device_id_type=pl.DeviceIdType.MESH,
            )
            copy.start()
            started.append(copy)
            slot += 1
    for index, ((axis, form), src, dst) in enumerate(zip(kinds, ins, outs)):
        if form == "gather_rows":
            rows = src.shape[1]
            place = dst.at[:, pl.ds(pl.multiple_of(me[axis] * rows, rows), rows)]
        elif form == "gather":
            place = dst.at[me[axis]]
        else:
            continue
        copy = pltpu.make_async_copy(src, place, local_sem.at[index])
        copy.start()
        started.append(copy)
    for copy in started:
        copy.wait()


def exchange(ident, *items):
    sizes = {"tensor": lax.axis_size("tensor"), "dp": lax.axis_size("dp")}
    kinds = tuple((axis, form) for axis, form, _ in items)
    shapes = []
    for axis, form, array in items:
        size = sizes[axis]
        if form == "gather_rows":
            shape = (array.shape[0], array.shape[1] * size, array.shape[2])
        elif form == "gather":
            shape = (size,) + array.shape
        elif form == "scatter_rows":
            shape = (size - 1, array.shape[0], array.shape[1] // size, array.shape[2])
        else:
            shape = (size - 1,) + array.shape[1:]
        shapes.append(jax.ShapeDtypeStruct(shape, array.dtype))
    copy_count = sum(sizes[axis] - 1 for axis, _ in kinds)
    return pl.pallas_call(
        functools.partial(exchange_body, kinds, sizes, copy_count),
        out_shape=shapes,
        in_specs=[pl.BlockSpec(memory_space=pl.ANY)] * len(items),
        out_specs=[pl.BlockSpec(memory_space=pl.ANY)] * len(items),
        scratch_shapes=[
            pltpu.SemaphoreType.DMA((copy_count,)),
            pltpu.SemaphoreType.DMA((copy_count,)),
            pltpu.SemaphoreType.DMA((len(items),)),
        ],
        compiler_params=pltpu.CompilerParams(collective_id=ident, has_side_effects=True),
    )(*[array for _, _, array in items])


def shift_tensor(array, step):
    size = lax.axis_size("tensor")
    return lax.ppermute(array, "tensor", [(i, (i + step) % size) for i in range(size)])


def scatter_async(piece, rows):
    size, index = lax.axis_size("tensor"), lax.axis_index("tensor")
    parts = [
        shift_tensor(
            lax.dynamic_slice_in_dim(piece, lax.rem(index + step, size) * rows, rows, 1), step
        )
        for step in range(1, size)
    ]
    own = lax.dynamic_slice_in_dim(piece, index * rows, rows, 1)
    return sum(part.astype(jnp.float32) for part in [own] + parts)


def place_rows(parts):
    size, index = len(parts), lax.axis_index("tensor")
    rows = parts[0].shape[1]
    whole = jnp.zeros(parts[0].shape[:1] + (rows * size,) + parts[0].shape[2:], parts[0].dtype)
    for step, part in enumerate(parts):
        source = lax.rem(index - step + size, size)
        whole = lax.dynamic_update_slice_in_dim(whole, part, source * rows, 1)
    return whole


def sum_rows(piece, arrived, start):
    own = lax.dynamic_slice_in_dim(piece, start, arrived.shape[2], 1).astype(jnp.float32)
    return own + jnp.sum(arrived.astype(jnp.float32), axis=0)


def sum_blocks(pieces, arrived, index):
    own = lax.dynamic_index_in_dim(pieces, index, 0, keepdims=False).astype(jnp.float32)
    return own + jnp.sum(arrived.astype(jnp.float32), axis=0)


def per_device(
    latents,
    conditioning,
    live_counts,
    ada_weight,
    ada_bias,
    qkv_weight,
    qv_bias,
    proj_weight,
    proj_bias,
    dense1_weight,
    dense1_bias,
    dense2_weight,
    dense2_bias,
    cotangent,
):
    lat_cap, seq_len, width = latents.shape
    head_count = qkv_weight.shape[2] // HD
    local_width = head_count * HD
    local_cols = ada_weight.shape[1]
    local_hidden = dense1_weight.shape[1]
    tensor_count = lax.axis_size("tensor")
    tensor_index = lax.axis_index("tensor")
    dp_count = lax.axis_size("dp")
    dp_index = lax.axis_index("dp")
    rows_dev = seq_len // tensor_count
    row_start = tensor_index * rows_dev
    scale_qk = HD ** (-0.5)
    live_mask = (jnp.arange(lat_cap) < live_counts[0]).astype(jnp.float32)[:, None, None]
    cond_f = conditioning.astype(jnp.float32)
    silu_b = to_half(jax.nn.silu(cond_f))
    mod_part = jnp.dot(silu_b, ada_weight, preferred_element_type=jnp.float32) + ada_bias
    mod_all, silu_all = exchange(
        1, ("tensor", "gather", mod_part), ("dp", "gather", silu_b.astype(jnp.float32))
    )
    modulation = jnp.swapaxes(mod_all, 0, 1).reshape(lat_cap, 6 * width)
    blocks = modulation.reshape(lat_cap, 6, width)[:, :, None, :]
    shift_one, scale_one, gate_one = (blocks[:, 0], blocks[:, 1], blocks[:, 2])
    shift_two, scale_two, gate_two = (blocks[:, 3], blocks[:, 4], blocks[:, 5])
    tokens_f = latents.astype(jnp.float32)
    norm_one, recip_one = norm_rows(tokens_f)
    h_one = to_half(norm_one * (1.0 + scale_one) + shift_one)
    qkv_rows = contract_lowprec("lsd,dce->lsce", h_one, qkv_weight)
    queries = to_half(qkv_rows[:, :, 0] + qv_bias[0]).reshape(lat_cap, seq_len, head_count, HD)
    key_rows = to_half(qkv_rows[:, :, 1]).reshape(lat_cap, seq_len, head_count, HD)
    value_rows = to_half(qkv_rows[:, :, 2] + qv_bias[1]).reshape(lat_cap, seq_len, head_count, HD)
    scores = contract_lowprec("lqhe,lkhe->lhqk", queries, key_rows) * scale_qk
    log_total = jax.nn.logsumexp(scores, axis=-1, keepdims=True)
    probs_b = to_half(jnp.exp(scores - log_total))
    attended = to_half(contract_lowprec("lhqk,lkhe->lqhe", probs_b, value_rows)).reshape(
        lat_cap, seq_len, local_width
    )
    attn_part = to_half(contract_lowprec("lsd,de->lse", attended, proj_weight))
    (attn_arrived,) = exchange(2, ("tensor", "scatter_rows", attn_part))
    attn_branch = sum_rows(attn_part, attn_arrived, row_start) + proj_bias
    tokens_own = lax.dynamic_slice_in_dim(tokens_f, row_start, rows_dev, 1)
    x_one = tokens_own + gate_one * attn_branch
    norm_two, recip_two = norm_rows(x_one)
    hidden_own = to_half(norm_two * (1.0 + scale_two) + shift_two)
    (hidden_second,) = exchange(3, ("tensor", "gather_rows", hidden_own))
    preactivation_rows = contract_lowprec("kow,wz->koz", hidden_second, dense1_weight) + dense1_bias
    activation_lowprec = to_half(jax.nn.gelu(preactivation_rows, approximate=True))
    perceptron_piece = to_half(contract_lowprec("jqv,vg->jqg", activation_lowprec, dense2_weight))
    perceptron_sum = scatter_async(perceptron_piece, rows_dev)
    dmlp = gate_two * (live_mask * cotangent.astype(jnp.float32))
    perceptron_gradient_lowprec = to_half(dmlp)
    grad_fc2_part = jnp.sum(dmlp, axis=(0, 1))
    dense2_gradient = to_half(
        contract_lowprec("kbi,kby->iy", perceptron_gradient_lowprec, activation_lowprec)
    ).reshape(dp_count, width // dp_count, local_hidden)
    activation_gradient = contract_lowprec(
        "vug,bg->vub", perceptron_gradient_lowprec, dense2_weight
    )
    dpre = activation_gradient * gelu_slope(preactivation_rows)
    preactivation_gradient_lowprec = to_half(dpre)
    dense1_gradient = to_half(
        contract_lowprec("qmw,qmx->wx", hidden_second, preactivation_gradient_lowprec)
    ).reshape(dp_count, width // dp_count, local_hidden)
    grad_fc1_b = jnp.sum(dpre, axis=(0, 1))
    hidden_gradient_piece = to_half(
        contract_lowprec("hnb,jb->hnj", preactivation_gradient_lowprec, dense1_weight)
    )
    hidden_arrived, fc1_arrived = exchange(
        4,
        ("tensor", "scatter_rows", hidden_gradient_piece),
        ("dp", "scatter", dense1_gradient),
    )
    summed_fc1 = sum_blocks(dense1_gradient, fc1_arrived, dp_index)
    hidden_second_gradient = sum_rows(hidden_gradient_piece, hidden_arrived, row_start)
    cot_own = lax.dynamic_slice_in_dim(cotangent, row_start, rows_dev, 1)
    grad_out = live_mask * cot_own.astype(jnp.float32)
    dscale_two = jnp.sum(hidden_second_gradient * norm_two, axis=1)
    dshift_two = jnp.sum(hidden_second_gradient, axis=1)
    dx_one = grad_out + norm_back(hidden_second_gradient * (1.0 + scale_two), norm_two, recip_two)
    dattn = gate_one * dx_one
    dgate_one = jnp.sum(dx_one * attn_branch, axis=1)
    dattn_own_b = to_half(dattn)
    grad_proj_part = jnp.sum(dattn, axis=(0, 1))
    dattn_b, fc2_arrived = exchange(
        5, ("tensor", "gather_rows", dattn_own_b), ("dp", "scatter", dense2_gradient)
    )
    summed_fc2 = sum_blocks(dense2_gradient, fc2_arrived, dp_index).T
    perceptron_branch = perceptron_sum + dense2_bias
    output_own = to_half(live_mask * (x_one + gate_two * perceptron_branch))
    dgate_two = jnp.sum(grad_out * perceptron_branch, axis=1)
    output_own, dattn_b = lax.optimization_barrier((output_own, dattn_b))
    parts = [output_own] + [shift_tensor(output_own, step) for step in range(1, tensor_count)]
    grad_proj = contract_lowprec("lse,lsd->ed", dattn_b, attended)
    dattended = to_half(contract_lowprec("lse,de->lsd", dattn_b, proj_weight)).reshape(
        lat_cap, seq_len, head_count, HD
    )
    scores_again = contract_lowprec("lqhe,lkhe->lhqk", queries, key_rows) * scale_qk
    probs = jnp.exp(scores_again - log_total)
    probs_again = to_half(probs)
    dprobs = contract_lowprec("lqhe,lkhe->lhqk", dattended, value_rows)
    delta = jnp.sum(probs * dprobs, axis=-1, keepdims=True)
    dscores_b = to_half(probs * (dprobs - delta) * scale_qk)
    parts[1 % tensor_count], dscores_b = lax.optimization_barrier((parts[1 % tensor_count], dscores_b))
    dquery = contract_lowprec("lhqk,lkhe->lqhe", dscores_b, key_rows).reshape(
        lat_cap, seq_len, local_width
    )
    dkey = contract_lowprec("lhqk,lqhe->lkhe", dscores_b, queries).reshape(
        lat_cap, seq_len, local_width
    )
    dvalue = contract_lowprec("lhqk,lqhe->lkhe", probs_again, dattended).reshape(
        lat_cap, seq_len, local_width
    )
    grad_qv = jnp.stack([jnp.sum(dquery, axis=(0, 1)), jnp.sum(dvalue, axis=(0, 1))], axis=0)
    dqkv_b = to_half(jnp.stack([dquery, dkey, dvalue], axis=2))
    parts[2 % tensor_count], dqkv_b = lax.optimization_barrier((parts[2 % tensor_count], dqkv_b))
    grad_qkv = contract_lowprec("lsd,lsce->dce", h_one, dqkv_b)
    dh_part_one = to_half(contract_lowprec("lsce,dce->lsd", dqkv_b, qkv_weight))
    parts[3 % tensor_count], dh_part_one = lax.optimization_barrier((parts[3 % tensor_count], dh_part_one))
    block_output = place_rows(parts)
    attn_gradient = jnp.concatenate(
        [to_half(grad_qkv).reshape(width, 3 * local_width), to_half(grad_proj)], axis=1
    ).reshape(dp_count, width // dp_count, 4 * local_width)
    dh_arrived, attn_gradient_arrived = exchange(
        6, ("tensor", "scatter_rows", dh_part_one), ("dp", "scatter", attn_gradient)
    )
    summed_attn = sum_blocks(attn_gradient, attn_gradient_arrived, dp_index)
    summed_qkv = summed_attn[:, : 3 * local_width].reshape(-1, 3, local_width)
    summed_proj = summed_attn[:, 3 * local_width :].T
    dh_one = sum_rows(dh_part_one, dh_arrived, row_start)
    norm_one_own = lax.dynamic_slice_in_dim(norm_one, row_start, rows_dev, 1)
    recip_one_own = lax.dynamic_slice_in_dim(recip_one, row_start, rows_dev, 1)
    dscale_one = jnp.sum(dh_one * norm_one_own, axis=1)
    dshift_one = jnp.sum(dh_one, axis=1)
    grad_own = dx_one + norm_back(dh_one * (1.0 + scale_one), norm_one_own, recip_one_own)
    stats_own = jnp.concatenate(
        [
            jnp.stack(
                [dshift_one, dscale_one, dgate_one, dshift_two, dscale_two, dgate_two], axis=1
            ).reshape(lat_cap * 6, width),
            grad_proj_part[None],
        ],
        axis=0,
    )
    grad_gathered, stats_all = exchange(
        7, ("tensor", "gather_rows", to_half(grad_own)), ("tensor", "gather", stats_own)
    )
    grad_latents = grad_gathered.astype(jnp.float32)
    stats_sum = jnp.sum(stats_all, axis=0)
    dmod = stats_sum[: lat_cap * 6].reshape(lat_cap, 6 * width)
    col_start = tensor_index * local_cols
    dmod_local = lax.dynamic_slice_in_dim(dmod, col_start, local_cols, 1)
    cond_part = contract_lowprec("le,de->ld", to_half(dmod_local), ada_weight)
    vectors = [
        dmod_local.reshape(-1),
        grad_qv.reshape(-1),
        grad_fc1_b,
        grad_fc2_part,
        stats_sum[lat_cap * 6],
    ]
    packed_all, cond_all = exchange(
        8, ("dp", "gather", jnp.concatenate(vectors)[None]), ("tensor", "gather", cond_part)
    )
    grad_conditioning = jnp.sum(cond_all, axis=0) * silu_slope(cond_f)
    packed_all = packed_all[:, 0]
    dmod_cols = lat_cap * local_cols
    dmod_all = packed_all[:, :dmod_cols].reshape(dp_count * lat_cap, local_cols)
    bias_ada = jnp.sum(dmod_all, axis=0)
    block = width // dp_count
    silu_own = lax.dynamic_slice_in_dim(
        to_half(silu_all).reshape(dp_count * lat_cap, width), dp_index * block, block, 1
    )
    summed_ada = contract_lowprec("ld,le->de", silu_own, to_half(dmod_all))
    totals = jnp.sum(packed_all[:, dmod_cols:], axis=0)
    bias_qv, bias_fc1, fc2_tot, proj_tot = jnp.split(
        totals,
        (2 * local_width, 2 * local_width + local_hidden, 2 * local_width + local_hidden + width),
    )
    bias_qv = bias_qv.reshape(2, local_width)
    return (
        block_output,
        grad_latents,
        grad_conditioning,
        summed_ada,
        bias_ada,
        summed_qkv,
        bias_qv,
        summed_proj,
        proj_tot,
        summed_fc1,
        bias_fc1,
        summed_fc2,
        fc2_tot,
    )


def solution(mesh):
    placed = (
        P("dp", None, None),
        P("dp", None),
        P("dp"),
        P(None, "tensor"),
        P("tensor"),
        P(None, None, "tensor"),
        P(None, "tensor"),
        P("tensor", None),
        P(),
        P(None, "tensor"),
        P("tensor"),
        P("tensor", None),
        P(),
        P("dp", None, None),
    )
    return jax.shard_map(
        per_device,
        mesh=mesh,
        in_specs=placed,
        out_specs=(
            P("dp", None, None),
            P("dp", None, None),
            P("dp", None),
            P("dp", "tensor"),
            P("tensor"),
            P("dp", None, "tensor"),
            P(None, "tensor"),
            P("tensor", "dp"),
            P(),
            P("dp", "tensor"),
            P("tensor"),
            P("tensor", "dp"),
            P(),
        ),
        check_vma=False,
    )
```

```python
import functools
import math

import jax
import jax.numpy as jnp
from jax import lax
from jax.experimental import pallas as pl
from jax.experimental.pallas import tpu as pltpu
from jax.sharding import PartitionSpec as P

HD = 64


EPS = 1e-06
GELU_C = math.sqrt(2.0 / math.pi)


def to_half(values):
    return values.astype(jnp.bfloat16)


def silu_slope(values):
    sig = jax.nn.sigmoid(values)
    return sig * (1.0 + values * (1.0 - sig))


def gelu_slope(values):
    tangent = jnp.tanh(GELU_C * (values + 0.044715 * values * values * values))
    return 0.5 * (1.0 + tangent) + 0.5 * values * (1.0 - tangent * tangent) * GELU_C * (
        1.0 + 3.0 * 0.044715 * values * values
    )


def norm_rows(values):
    center = values - jnp.mean(values, axis=-1, keepdims=True)
    recip = lax.rsqrt(jnp.mean(center * center, axis=-1, keepdims=True) + EPS)
    return (center * recip, recip)


def norm_back(grad_norm, normed, recip):
    return recip * (
        grad_norm
        - jnp.mean(grad_norm, axis=-1, keepdims=True)
        - normed * jnp.mean(grad_norm * normed, axis=-1, keepdims=True)
    )


def contract_lowprec(form, left, right):
    return jnp.einsum(form, left, right, preferred_element_type=jnp.float32)


def exchange_body(kinds, sizes, copy_count, *refs):
    count = len(kinds)
    ins, outs = refs[:count], refs[count : 2 * count]
    send_sem, recv_sem, local_sem = refs[2 * count :]
    axes = [axis for axis in ("tensor", "dp") if any(k[0] == axis for k in kinds)]
    me = {axis: lax.axis_index(axis) for axis in axes}
    barrier = pltpu.get_barrier_semaphore()
    peers = 0
    for axis in axes:
        for step in range(1, sizes[axis]):
            pl.semaphore_signal(
                barrier,
                inc=1,
                device_id={axis: lax.rem(me[axis] + step, sizes[axis])},
                device_id_type=pl.DeviceIdType.MESH,
            )
            peers += 1
    pl.semaphore_wait(barrier, peers)
    started = []
    slot = 0
    for step in range(1, max(sizes.values())):
        for (axis, form), src, dst in zip(kinds, ins, outs):
            size = sizes[axis]
            if step >= size:
                continue
            target = lax.rem(me[axis] + step, size)
            if form == "gather_rows":
                rows = src.shape[1]
                source = src
                place = dst.at[:, pl.ds(pl.multiple_of(me[axis] * rows, rows), rows)]
            elif form == "gather":
                source, place = src, dst.at[me[axis]]
            elif form == "scatter_rows":
                rows = src.shape[1] // size
                source = src.at[:, pl.ds(pl.multiple_of(target * rows, rows), rows)]
                place = dst.at[step - 1]
            else:
                source, place = src.at[target], dst.at[step - 1]
            copy = pltpu.make_async_remote_copy(
                src_ref=source,
                dst_ref=place,
                send_sem=send_sem.at[slot],
                recv_sem=recv_sem.at[slot],
                device_id={axis: target},
                device_id_type=pl.DeviceIdType.MESH,
            )
            copy.start()
            started.append(copy)
            slot += 1
    for index, ((axis, form), src, dst) in enumerate(zip(kinds, ins, outs)):
        if form == "gather_rows":
            rows = src.shape[1]
            place = dst.at[:, pl.ds(pl.multiple_of(me[axis] * rows, rows), rows)]
        elif form == "gather":
            place = dst.at[me[axis]]
        else:
            continue
        copy = pltpu.make_async_copy(src, place, local_sem.at[index])
        copy.start()
        started.append(copy)
    for copy in started:
        copy.wait()


def exchange(ident, *items):
    sizes = {"tensor": lax.axis_size("tensor"), "dp": lax.axis_size("dp")}
    kinds = tuple((axis, form) for axis, form, _ in items)
    shapes = []
    for axis, form, array in items:
        size = sizes[axis]
        if form == "gather_rows":
            shape = (array.shape[0], array.shape[1] * size, array.shape[2])
        elif form == "gather":
            shape = (size,) + array.shape
        elif form == "scatter_rows":
            shape = (size - 1, array.shape[0], array.shape[1] // size, array.shape[2])
        else:
            shape = (size - 1,) + array.shape[1:]
        shapes.append(jax.ShapeDtypeStruct(shape, array.dtype))
    copy_count = sum(sizes[axis] - 1 for axis, _ in kinds)
    return pl.pallas_call(
        functools.partial(exchange_body, kinds, sizes, copy_count),
        out_shape=shapes,
        in_specs=[pl.BlockSpec(memory_space=pl.ANY)] * len(items),
        out_specs=[pl.BlockSpec(memory_space=pl.ANY)] * len(items),
        scratch_shapes=[
            pltpu.SemaphoreType.DMA((copy_count,)),
            pltpu.SemaphoreType.DMA((copy_count,)),
            pltpu.SemaphoreType.DMA((len(items),)),
        ],
        compiler_params=pltpu.CompilerParams(collective_id=ident, has_side_effects=True),
    )(*[array for _, _, array in items])


def shift_tensor(array, step):
    size = lax.axis_size("tensor")
    return lax.ppermute(array, "tensor", [(i, (i + step) % size) for i in range(size)])


def scatter_async(piece, rows):
    size, index = lax.axis_size("tensor"), lax.axis_index("tensor")
    parts = [
        shift_tensor(
            lax.dynamic_slice_in_dim(piece, lax.rem(index + step, size) * rows, rows, 1), step
        )
        for step in range(1, size)
    ]
    own = lax.dynamic_slice_in_dim(piece, index * rows, rows, 1)
    return sum(part.astype(jnp.float32) for part in [own] + parts)


def place_rows(parts):
    size, index = len(parts), lax.axis_index("tensor")
    rows = parts[0].shape[1]
    whole = jnp.zeros(parts[0].shape[:1] + (rows * size,) + parts[0].shape[2:], parts[0].dtype)
    for step, part in enumerate(parts):
        source = lax.rem(index - step + size, size)
        whole = lax.dynamic_update_slice_in_dim(whole, part, source * rows, 1)
    return whole


def sum_rows(piece, arrived, start):
    own = lax.dynamic_slice_in_dim(piece, start, arrived.shape[2], 1).astype(jnp.float32)
    return own + jnp.sum(arrived.astype(jnp.float32), axis=0)


def sum_blocks(pieces, arrived, index):
    own = lax.dynamic_index_in_dim(pieces, index, 0, keepdims=False).astype(jnp.float32)
    return own + jnp.sum(arrived.astype(jnp.float32), axis=0)


def per_device(
    latents,
    conditioning,
    live_counts,
    ada_weight,
    ada_bias,
    qkv_weight,
    qv_bias,
    proj_weight,
    proj_bias,
    dense1_weight,
    dense1_bias,
    dense2_weight,
    dense2_bias,
    cotangent,
):
    lat_cap, seq_len, width = latents.shape
    head_count = qkv_weight.shape[2] // HD
    local_width = head_count * HD
    local_cols = ada_weight.shape[1]
    local_hidden = dense1_weight.shape[1]
    tensor_count = lax.axis_size("tensor")
    tensor_index = lax.axis_index("tensor")
    dp_count = lax.axis_size("dp")
    dp_index = lax.axis_index("dp")
    rows_dev = seq_len // tensor_count
    row_start = tensor_index * rows_dev
    scale_qk = HD ** (-0.5)
    live_mask = (jnp.arange(lat_cap) < live_counts[0]).astype(jnp.float32)[:, None, None]
    cond_f = conditioning.astype(jnp.float32)
    silu_b = to_half(jax.nn.silu(cond_f))
    mod_part = jnp.dot(silu_b, ada_weight, preferred_element_type=jnp.float32) + ada_bias
    mod_all, silu_all = exchange(
        1, ("tensor", "gather", mod_part), ("dp", "gather", silu_b.astype(jnp.float32))
    )
    modulation = jnp.swapaxes(mod_all, 0, 1).reshape(lat_cap, 6 * width)
    blocks = modulation.reshape(lat_cap, 6, width)[:, :, None, :]
    shift_one, scale_one, gate_one = (blocks[:, 0], blocks[:, 1], blocks[:, 2])
    shift_two, scale_two, gate_two = (blocks[:, 3], blocks[:, 4], blocks[:, 5])
    tokens_f = latents.astype(jnp.float32)
    norm_one, recip_one = norm_rows(tokens_f)
    h_one = to_half(norm_one * (1.0 + scale_one) + shift_one)
    qkv_rows = contract_lowprec("lsd,dce->lsce", h_one, qkv_weight)
    queries = to_half(qkv_rows[:, :, 0] + qv_bias[0]).reshape(lat_cap, seq_len, head_count, HD)
    key_rows = to_half(qkv_rows[:, :, 1]).reshape(lat_cap, seq_len, head_count, HD)
    value_rows = to_half(qkv_rows[:, :, 2] + qv_bias[1]).reshape(lat_cap, seq_len, head_count, HD)
    scores = contract_lowprec("lqhe,lkhe->lhqk", queries, key_rows) * scale_qk
    log_total = jax.nn.logsumexp(scores, axis=-1, keepdims=True)
    probs_b = to_half(jnp.exp(scores - log_total))
    attended = to_half(contract_lowprec("lhqk,lkhe->lqhe", probs_b, value_rows)).reshape(
        lat_cap, seq_len, local_width
    )
    attn_part = to_half(contract_lowprec("lsd,de->lse", attended, proj_weight))
    (attn_arrived,) = exchange(2, ("tensor", "scatter_rows", attn_part))
    attn_branch = sum_rows(attn_part, attn_arrived, row_start) + proj_bias
    tokens_own = lax.dynamic_slice_in_dim(tokens_f, row_start, rows_dev, 1)
    x_one = tokens_own + gate_one * attn_branch
    norm_two, recip_two = norm_rows(x_one)
    hidden_own = to_half(norm_two * (1.0 + scale_two) + shift_two)
    (hidden_second,) = exchange(3, ("tensor", "gather_rows", hidden_own))
    preactivation_rows = contract_lowprec("kow,wz->koz", hidden_second, dense1_weight) + dense1_bias
    activation_lowprec = to_half(jax.nn.gelu(preactivation_rows, approximate=True))
    perceptron_piece = to_half(contract_lowprec("jqv,vg->jqg", activation_lowprec, dense2_weight))
    perceptron_sum = scatter_async(perceptron_piece, rows_dev)
    dmlp = gate_two * (live_mask * cotangent.astype(jnp.float32))
    perceptron_gradient_lowprec = to_half(dmlp)
    grad_fc2_part = jnp.sum(dmlp, axis=(0, 1))
    dense2_gradient = to_half(
        contract_lowprec("kbi,kby->iy", perceptron_gradient_lowprec, activation_lowprec)
    ).reshape(dp_count, width // dp_count, local_hidden)
    activation_gradient = contract_lowprec(
        "vug,bg->vub", perceptron_gradient_lowprec, dense2_weight
    )
    dpre = activation_gradient * gelu_slope(preactivation_rows)
    preactivation_gradient_lowprec = to_half(dpre)
    dense1_gradient = to_half(
        contract_lowprec("qmw,qmx->wx", hidden_second, preactivation_gradient_lowprec)
    ).reshape(dp_count, width // dp_count, local_hidden)
    grad_fc1_b = jnp.sum(dpre, axis=(0, 1))
    hidden_gradient_piece = to_half(
        contract_lowprec("hnb,jb->hnj", preactivation_gradient_lowprec, dense1_weight)
    )
    hidden_arrived, fc1_arrived = exchange(
        4,
        ("tensor", "scatter_rows", hidden_gradient_piece),
        ("dp", "scatter", dense1_gradient),
    )
    summed_fc1 = sum_blocks(dense1_gradient, fc1_arrived, dp_index)
    hidden_second_gradient = sum_rows(hidden_gradient_piece, hidden_arrived, row_start)
    cot_own = lax.dynamic_slice_in_dim(cotangent, row_start, rows_dev, 1)
    grad_out = live_mask * cot_own.astype(jnp.float32)
    dscale_two = jnp.sum(hidden_second_gradient * norm_two, axis=1)
    dshift_two = jnp.sum(hidden_second_gradient, axis=1)
    dx_one = grad_out + norm_back(hidden_second_gradient * (1.0 + scale_two), norm_two, recip_two)
    dattn = gate_one * dx_one
    dgate_one = jnp.sum(dx_one * attn_branch, axis=1)
    dattn_own_b = to_half(dattn)
    grad_proj_part = jnp.sum(dattn, axis=(0, 1))
    dattn_b, fc2_arrived = exchange(
        5, ("tensor", "gather_rows", dattn_own_b), ("dp", "scatter", dense2_gradient)
    )
    summed_fc2 = sum_blocks(dense2_gradient, fc2_arrived, dp_index).T
    perceptron_branch = perceptron_sum + dense2_bias
    output_own = to_half(live_mask * (x_one + gate_two * perceptron_branch))
    dgate_two = jnp.sum(grad_out * perceptron_branch, axis=1)
    output_own, dattn_b = lax.optimization_barrier((output_own, dattn_b))
    parts = [output_own] + [shift_tensor(output_own, step) for step in range(1, tensor_count)]
    grad_proj = contract_lowprec("lse,lsd->ed", dattn_b, attended)
    dattended = to_half(contract_lowprec("lse,de->lsd", dattn_b, proj_weight)).reshape(
        lat_cap, seq_len, head_count, HD
    )
    scores_again = contract_lowprec("lqhe,lkhe->lhqk", queries, key_rows) * scale_qk
    probs = jnp.exp(scores_again - log_total)
    probs_again = to_half(probs)
    dprobs = contract_lowprec("lqhe,lkhe->lhqk", dattended, value_rows)
    delta = jnp.sum(probs * dprobs, axis=-1, keepdims=True)
    dscores_b = to_half(probs * (dprobs - delta) * scale_qk)
    parts[1 % tensor_count], dscores_b = lax.optimization_barrier((parts[1 % tensor_count], dscores_b))
    dquery = contract_lowprec("lhqk,lkhe->lqhe", dscores_b, key_rows).reshape(
        lat_cap, seq_len, local_width
    )
    dkey = contract_lowprec("lhqk,lqhe->lkhe", dscores_b, queries).reshape(
        lat_cap, seq_len, local_width
    )
    dvalue = contract_lowprec("lhqk,lqhe->lkhe", probs_again, dattended).reshape(
        lat_cap, seq_len, local_width
    )
    grad_qv = jnp.stack([jnp.sum(dquery, axis=(0, 1)), jnp.sum(dvalue, axis=(0, 1))], axis=0)
    dqkv_b = to_half(jnp.stack([dquery, dkey, dvalue], axis=2))
    parts[2 % tensor_count], dqkv_b = lax.optimization_barrier((parts[2 % tensor_count], dqkv_b))
    grad_qkv = contract_lowprec("lsd,lsce->dce", h_one, dqkv_b)
    dh_part_one = to_half(contract_lowprec("lsce,dce->lsd", dqkv_b, qkv_weight))
    parts[3 % tensor_count], dh_part_one = lax.optimization_barrier((parts[3 % tensor_count], dh_part_one))
    block_output = place_rows(parts)
    attn_gradient = jnp.concatenate(
        [to_half(grad_qkv).reshape(width, 3 * local_width), to_half(grad_proj)], axis=1
    ).reshape(dp_count, width // dp_count, 4 * local_width)
    dh_arrived, attn_gradient_arrived = exchange(
        6, ("tensor", "scatter_rows", dh_part_one), ("dp", "scatter", attn_gradient)
    )
    summed_attn = sum_blocks(attn_gradient, attn_gradient_arrived, dp_index)
    summed_qkv = summed_attn[:, : 3 * local_width].reshape(-1, 3, local_width)
    summed_proj = summed_attn[:, 3 * local_width :].T
    dh_one = sum_rows(dh_part_one, dh_arrived, row_start)
    norm_one_own = lax.dynamic_slice_in_dim(norm_one, row_start, rows_dev, 1)
    recip_one_own = lax.dynamic_slice_in_dim(recip_one, row_start, rows_dev, 1)
    dscale_one = jnp.sum(dh_one * norm_one_own, axis=1)
    dshift_one = jnp.sum(dh_one, axis=1)
    grad_own = dx_one + norm_back(dh_one * (1.0 + scale_one), norm_one_own, recip_one_own)
    stats_own = jnp.stack(
        [dshift_one, dscale_one, dgate_one, dshift_two, dscale_two, dgate_two], axis=1
    ).reshape(lat_cap, tensor_count, local_cols)
    stats_own = jnp.swapaxes(stats_own, 0, 1)
    grad_gathered, stats_arrived, proj_all = exchange(
        7,
        ("tensor", "gather_rows", to_half(grad_own)),
        ("tensor", "scatter", stats_own),
        ("tensor", "gather", grad_proj_part[None]),
    )
    grad_latents = grad_gathered.astype(jnp.float32)
    dmod_local = sum_blocks(stats_own, stats_arrived, tensor_index)
    cond_part = contract_lowprec("le,de->ld", to_half(dmod_local), ada_weight)
    vectors = [
        dmod_local.reshape(-1),
        grad_qv.reshape(-1),
        grad_fc1_b,
        grad_fc2_part,
        jnp.sum(proj_all[:, 0], axis=0),
    ]
    packed_all, cond_all = exchange(
        8, ("dp", "gather", jnp.concatenate(vectors)[None]), ("tensor", "gather", cond_part)
    )
    grad_conditioning = jnp.sum(cond_all, axis=0) * silu_slope(cond_f)
    packed_all = packed_all[:, 0]
    dmod_cols = lat_cap * local_cols
    dmod_all = packed_all[:, :dmod_cols].reshape(dp_count * lat_cap, local_cols)
    bias_ada = jnp.sum(dmod_all, axis=0)
    block = width // dp_count
    silu_own = lax.dynamic_slice_in_dim(
        to_half(silu_all).reshape(dp_count * lat_cap, width), dp_index * block, block, 1
    )
    summed_ada = contract_lowprec("ld,le->de", silu_own, to_half(dmod_all))
    totals = jnp.sum(packed_all[:, dmod_cols:], axis=0)
    bias_qv, bias_fc1, fc2_tot, proj_tot = jnp.split(
        totals,
        (2 * local_width, 2 * local_width + local_hidden, 2 * local_width + local_hidden + width),
    )
    bias_qv = bias_qv.reshape(2, local_width)
    return (
        block_output,
        grad_latents,
        grad_conditioning,
        summed_ada,
        bias_ada,
        summed_qkv,
        bias_qv,
        summed_proj,
        proj_tot,
        summed_fc1,
        bias_fc1,
        summed_fc2,
        fc2_tot,
    )


def solution(mesh):
    placed = (
        P("dp", None, None),
        P("dp", None),
        P("dp"),
        P(None, "tensor"),
        P("tensor"),
        P(None, None, "tensor"),
        P(None, "tensor"),
        P("tensor", None),
        P(),
        P(None, "tensor"),
        P("tensor"),
        P("tensor", None),
        P(),
        P("dp", None, None),
    )
    return jax.shard_map(
        per_device,
        mesh=mesh,
        in_specs=placed,
        out_specs=(
            P("dp", None, None),
            P("dp", None, None),
            P("dp", None),
            P("dp", "tensor"),
            P("tensor"),
            P("dp", None, "tensor"),
            P(None, "tensor"),
            P("tensor", "dp"),
            P(),
            P("dp", "tensor"),
            P("tensor"),
            P("tensor", "dp"),
            P(),
        ),
        check_vma=False,
    )
```

```python
import functools
import math

import jax
import jax.numpy as jnp
from jax import lax
from jax.experimental import pallas as pl
from jax.experimental.pallas import tpu as pltpu
from jax.sharding import PartitionSpec as P

HD = 64


EPS = 1e-06
GELU_C = math.sqrt(2.0 / math.pi)


def to_half(values):
    return values.astype(jnp.bfloat16)


def silu_slope(values):
    sig = jax.nn.sigmoid(values)
    return sig * (1.0 + values * (1.0 - sig))


def gelu_slope(values):
    tangent = jnp.tanh(GELU_C * (values + 0.044715 * values * values * values))
    return 0.5 * (1.0 + tangent) + 0.5 * values * (1.0 - tangent * tangent) * GELU_C * (
        1.0 + 3.0 * 0.044715 * values * values
    )


def norm_rows(values):
    center = values - jnp.mean(values, axis=-1, keepdims=True)
    recip = lax.rsqrt(jnp.mean(center * center, axis=-1, keepdims=True) + EPS)
    return (center * recip, recip)


def norm_back(grad_norm, normed, recip):
    return recip * (
        grad_norm
        - jnp.mean(grad_norm, axis=-1, keepdims=True)
        - normed * jnp.mean(grad_norm * normed, axis=-1, keepdims=True)
    )


def contract_lowprec(form, left, right):
    return jnp.einsum(form, left, right, preferred_element_type=jnp.float32)


def exchange_body(kinds, sizes, copy_count, *refs):
    count = len(kinds)
    ins, outs = refs[:count], refs[count : 2 * count]
    send_sem, recv_sem, local_sem = refs[2 * count :]
    axes = [axis for axis in ("tensor", "dp") if any(k[0] == axis for k in kinds)]
    me = {axis: lax.axis_index(axis) for axis in axes}
    barrier = pltpu.get_barrier_semaphore()
    peers = 0
    for axis in axes:
        for step in range(1, sizes[axis]):
            pl.semaphore_signal(
                barrier,
                inc=1,
                device_id={axis: lax.rem(me[axis] + step, sizes[axis])},
                device_id_type=pl.DeviceIdType.MESH,
            )
            peers += 1
    pl.semaphore_wait(barrier, peers)
    started = []
    slot = 0
    for step in range(1, max(sizes.values())):
        for (axis, form), src, dst in zip(kinds, ins, outs):
            size = sizes[axis]
            if step >= size:
                continue
            target = lax.rem(me[axis] + step, size)
            if form == "gather_rows":
                rows = src.shape[1]
                source = src
                place = dst.at[:, pl.ds(pl.multiple_of(me[axis] * rows, rows), rows)]
            elif form == "gather":
                source, place = src, dst.at[me[axis]]
            elif form == "scatter_rows":
                rows = src.shape[1] // size
                source = src.at[:, pl.ds(pl.multiple_of(target * rows, rows), rows)]
                place = dst.at[step - 1]
            else:
                source, place = src.at[target], dst.at[step - 1]
            copy = pltpu.make_async_remote_copy(
                src_ref=source,
                dst_ref=place,
                send_sem=send_sem.at[slot],
                recv_sem=recv_sem.at[slot],
                device_id={axis: target},
                device_id_type=pl.DeviceIdType.MESH,
            )
            copy.start()
            started.append(copy)
            slot += 1
    for index, ((axis, form), src, dst) in enumerate(zip(kinds, ins, outs)):
        if form == "gather_rows":
            rows = src.shape[1]
            place = dst.at[:, pl.ds(pl.multiple_of(me[axis] * rows, rows), rows)]
        elif form == "gather":
            place = dst.at[me[axis]]
        else:
            continue
        copy = pltpu.make_async_copy(src, place, local_sem.at[index])
        copy.start()
        started.append(copy)
    for copy in started:
        copy.wait()


def exchange(ident, *items):
    sizes = {"tensor": lax.axis_size("tensor"), "dp": lax.axis_size("dp")}
    kinds = tuple((axis, form) for axis, form, _ in items)
    shapes = []
    for axis, form, array in items:
        size = sizes[axis]
        if form == "gather_rows":
            shape = (array.shape[0], array.shape[1] * size, array.shape[2])
        elif form == "gather":
            shape = (size,) + array.shape
        elif form == "scatter_rows":
            shape = (size - 1, array.shape[0], array.shape[1] // size, array.shape[2])
        else:
            shape = (size - 1,) + array.shape[1:]
        shapes.append(jax.ShapeDtypeStruct(shape, array.dtype))
    copy_count = sum(sizes[axis] - 1 for axis, _ in kinds)
    return pl.pallas_call(
        functools.partial(exchange_body, kinds, sizes, copy_count),
        out_shape=shapes,
        in_specs=[pl.BlockSpec(memory_space=pl.ANY)] * len(items),
        out_specs=[pl.BlockSpec(memory_space=pl.ANY)] * len(items),
        scratch_shapes=[
            pltpu.SemaphoreType.DMA((copy_count,)),
            pltpu.SemaphoreType.DMA((copy_count,)),
            pltpu.SemaphoreType.DMA((len(items),)),
        ],
        compiler_params=pltpu.CompilerParams(collective_id=ident, has_side_effects=True),
    )(*[array for _, _, array in items])


def shift_tensor(array, step):
    size = lax.axis_size("tensor")
    return lax.ppermute(array, "tensor", [(i, (i + step) % size) for i in range(size)])


def scatter_async(piece, rows):
    size, index = lax.axis_size("tensor"), lax.axis_index("tensor")
    parts = [
        shift_tensor(
            lax.dynamic_slice_in_dim(piece, lax.rem(index + step, size) * rows, rows, 1), step
        )
        for step in range(1, size)
    ]
    own = lax.dynamic_slice_in_dim(piece, index * rows, rows, 1)
    return sum(part.astype(jnp.float32) for part in [own] + parts)


def place_rows(parts):
    size, index = len(parts), lax.axis_index("tensor")
    rows = parts[0].shape[1]
    whole = jnp.zeros(parts[0].shape[:1] + (rows * size,) + parts[0].shape[2:], parts[0].dtype)
    for step, part in enumerate(parts):
        source = lax.rem(index - step + size, size)
        whole = lax.dynamic_update_slice_in_dim(whole, part, source * rows, 1)
    return whole


def sum_rows(piece, arrived, start):
    own = lax.dynamic_slice_in_dim(piece, start, arrived.shape[2], 1).astype(jnp.float32)
    return own + jnp.sum(arrived.astype(jnp.float32), axis=0)


def sum_blocks(pieces, arrived, index):
    own = lax.dynamic_index_in_dim(pieces, index, 0, keepdims=False).astype(jnp.float32)
    return own + jnp.sum(arrived.astype(jnp.float32), axis=0)


def per_device(
    latents,
    conditioning,
    live_counts,
    ada_weight,
    ada_bias,
    qkv_weight,
    qv_bias,
    proj_weight,
    proj_bias,
    dense1_weight,
    dense1_bias,
    dense2_weight,
    dense2_bias,
    cotangent,
):
    lat_cap, seq_len, width = latents.shape
    head_count = qkv_weight.shape[2] // HD
    local_width = head_count * HD
    local_cols = ada_weight.shape[1]
    local_hidden = dense1_weight.shape[1]
    tensor_count = lax.axis_size("tensor")
    tensor_index = lax.axis_index("tensor")
    dp_count = lax.axis_size("dp")
    dp_index = lax.axis_index("dp")
    rows_dev = seq_len // tensor_count
    row_start = tensor_index * rows_dev
    scale_qk = HD ** (-0.5)
    live_mask = (jnp.arange(lat_cap) < live_counts[0]).astype(jnp.float32)[:, None, None]
    cond_f = conditioning.astype(jnp.float32)
    silu_b = to_half(jax.nn.silu(cond_f))
    mod_part = jnp.dot(silu_b, ada_weight, preferred_element_type=jnp.float32) + ada_bias
    mod_all, silu_all = exchange(
        1, ("tensor", "gather", mod_part), ("dp", "gather", silu_b.astype(jnp.float32))
    )
    modulation = jnp.swapaxes(mod_all, 0, 1).reshape(lat_cap, 6 * width)
    blocks = modulation.reshape(lat_cap, 6, width)[:, :, None, :]
    shift_one, scale_one, gate_one = (blocks[:, 0], blocks[:, 1], blocks[:, 2])
    shift_two, scale_two, gate_two = (blocks[:, 3], blocks[:, 4], blocks[:, 5])
    tokens_f = latents.astype(jnp.float32)
    norm_one, recip_one = norm_rows(tokens_f)
    h_one = to_half(norm_one * (1.0 + scale_one) + shift_one)
    qkv_rows = contract_lowprec("lsd,dce->lsce", h_one, qkv_weight)
    queries = to_half(qkv_rows[:, :, 0] + qv_bias[0]).reshape(lat_cap, seq_len, head_count, HD)
    key_rows = to_half(qkv_rows[:, :, 1]).reshape(lat_cap, seq_len, head_count, HD)
    value_rows = to_half(qkv_rows[:, :, 2] + qv_bias[1]).reshape(lat_cap, seq_len, head_count, HD)
    scores = contract_lowprec("lqhe,lkhe->lhqk", queries, key_rows) * scale_qk
    log_total = jax.nn.logsumexp(scores, axis=-1, keepdims=True)
    probs_b = to_half(jnp.exp(scores - log_total))
    attended = to_half(contract_lowprec("lhqk,lkhe->lqhe", probs_b, value_rows)).reshape(
        lat_cap, seq_len, local_width
    )
    attn_part = to_half(contract_lowprec("lsd,de->lse", attended, proj_weight))
    (attn_arrived,) = exchange(2, ("tensor", "scatter_rows", attn_part))
    attn_branch = sum_rows(attn_part, attn_arrived, row_start) + proj_bias
    tokens_own = lax.dynamic_slice_in_dim(tokens_f, row_start, rows_dev, 1)
    x_one = tokens_own + gate_one * attn_branch
    norm_two, recip_two = norm_rows(x_one)
    hidden_own = to_half(norm_two * (1.0 + scale_two) + shift_two)
    (hidden_second,) = exchange(3, ("tensor", "gather_rows", hidden_own))
    preactivation_rows = contract_lowprec("kow,wz->koz", hidden_second, dense1_weight) + dense1_bias
    activation_lowprec = to_half(jax.nn.gelu(preactivation_rows, approximate=True))
    perceptron_piece = to_half(contract_lowprec("jqv,vg->jqg", activation_lowprec, dense2_weight))
    perceptron_sum = scatter_async(perceptron_piece, rows_dev)
    dmlp = gate_two * (live_mask * cotangent.astype(jnp.float32))
    perceptron_gradient_lowprec = to_half(dmlp)
    grad_fc2_part = jnp.sum(dmlp, axis=(0, 1))
    dense2_gradient = to_half(
        contract_lowprec("kbi,kby->iy", perceptron_gradient_lowprec, activation_lowprec)
    ).reshape(dp_count, width // dp_count, local_hidden)
    activation_gradient = contract_lowprec(
        "vug,bg->vub", perceptron_gradient_lowprec, dense2_weight
    )
    dpre = activation_gradient * gelu_slope(preactivation_rows)
    preactivation_gradient_lowprec = to_half(dpre)
    dense1_gradient = to_half(
        contract_lowprec("qmw,qmx->wx", hidden_second, preactivation_gradient_lowprec)
    ).reshape(dp_count, width // dp_count, local_hidden)
    grad_fc1_b = jnp.sum(dpre, axis=(0, 1))
    hidden_gradient_piece = to_half(
        contract_lowprec("hnb,jb->hnj", preactivation_gradient_lowprec, dense1_weight)
    )
    hidden_arrived, fc1_arrived = exchange(
        4,
        ("tensor", "scatter_rows", hidden_gradient_piece),
        ("dp", "scatter", dense1_gradient),
    )
    summed_fc1 = sum_blocks(dense1_gradient, fc1_arrived, dp_index)
    hidden_second_gradient = sum_rows(hidden_gradient_piece, hidden_arrived, row_start)
    cot_own = lax.dynamic_slice_in_dim(cotangent, row_start, rows_dev, 1)
    grad_out = live_mask * cot_own.astype(jnp.float32)
    dscale_two = jnp.sum(hidden_second_gradient * norm_two, axis=1)
    dshift_two = jnp.sum(hidden_second_gradient, axis=1)
    dx_one = grad_out + norm_back(hidden_second_gradient * (1.0 + scale_two), norm_two, recip_two)
    dattn = gate_one * dx_one
    dgate_one = jnp.sum(dx_one * attn_branch, axis=1)
    dattn_own_b = to_half(dattn)
    grad_proj_part = jnp.sum(dattn, axis=(0, 1))
    dattn_b, fc2_arrived = exchange(
        5, ("tensor", "gather_rows", dattn_own_b), ("dp", "scatter", dense2_gradient)
    )
    summed_fc2 = sum_blocks(dense2_gradient, fc2_arrived, dp_index).T
    perceptron_branch = perceptron_sum + dense2_bias
    output_own = to_half(live_mask * (x_one + gate_two * perceptron_branch))
    dgate_two = jnp.sum(grad_out * perceptron_branch, axis=1)
    output_own, dattn_b = lax.optimization_barrier((output_own, dattn_b))
    parts = [output_own] + [shift_tensor(output_own, step) for step in range(1, tensor_count)]
    grad_proj = contract_lowprec("lse,lsd->ed", dattn_b, attended)
    dattended = to_half(contract_lowprec("lse,de->lsd", dattn_b, proj_weight)).reshape(
        lat_cap, seq_len, head_count, HD
    )
    scores_again = contract_lowprec("lqhe,lkhe->lhqk", queries, key_rows) * scale_qk
    probs = jnp.exp(scores_again - log_total)
    probs_again = to_half(probs)
    dprobs = contract_lowprec("lqhe,lkhe->lhqk", dattended, value_rows)
    delta = jnp.sum(probs * dprobs, axis=-1, keepdims=True)
    dscores_b = to_half(probs * (dprobs - delta) * scale_qk)
    parts[1 % tensor_count], dscores_b = lax.optimization_barrier((parts[1 % tensor_count], dscores_b))
    dquery = contract_lowprec("lhqk,lkhe->lqhe", dscores_b, key_rows).reshape(
        lat_cap, seq_len, local_width
    )
    dkey = contract_lowprec("lhqk,lqhe->lkhe", dscores_b, queries).reshape(
        lat_cap, seq_len, local_width
    )
    dvalue = contract_lowprec("lhqk,lqhe->lkhe", probs_again, dattended).reshape(
        lat_cap, seq_len, local_width
    )
    grad_qv = jnp.stack([jnp.sum(dquery, axis=(0, 1)), jnp.sum(dvalue, axis=(0, 1))], axis=0)
    dqkv_b = to_half(jnp.concatenate([dquery, dkey, dvalue], axis=2))
    parts[2 % tensor_count], dqkv_b = lax.optimization_barrier((parts[2 % tensor_count], dqkv_b))
    grad_qkv = contract_lowprec("lsd,lsf->df", h_one, dqkv_b)
    dh_part_one = to_half(contract_lowprec(
        "lsf,df->lsd", dqkv_b, qkv_weight.reshape(width, 3 * local_width)
    ))
    parts[3 % tensor_count], dh_part_one = lax.optimization_barrier((parts[3 % tensor_count], dh_part_one))
    block_output = place_rows(parts)
    qkv_blocks = to_half(grad_qkv).reshape(dp_count, width // dp_count, 3 * local_width)
    proj_blocks = to_half(grad_proj).reshape(dp_count, width // dp_count, local_width)
    dh_arrived, qkv_arrived, proj_arrived = exchange(
        6,
        ("tensor", "scatter_rows", dh_part_one),
        ("dp", "scatter", qkv_blocks),
        ("dp", "scatter", proj_blocks),
    )
    summed_qkv = sum_blocks(qkv_blocks, qkv_arrived, dp_index).reshape(-1, 3, local_width)
    summed_proj = sum_blocks(proj_blocks, proj_arrived, dp_index).T
    dh_one = sum_rows(dh_part_one, dh_arrived, row_start)
    norm_one_own = lax.dynamic_slice_in_dim(norm_one, row_start, rows_dev, 1)
    recip_one_own = lax.dynamic_slice_in_dim(recip_one, row_start, rows_dev, 1)
    dscale_one = jnp.sum(dh_one * norm_one_own, axis=1)
    dshift_one = jnp.sum(dh_one, axis=1)
    grad_own = dx_one + norm_back(dh_one * (1.0 + scale_one), norm_one_own, recip_one_own)
    stats_own = jnp.stack(
        [dshift_one, dscale_one, dgate_one, dshift_two, dscale_two, dgate_two], axis=1
    ).reshape(lat_cap, tensor_count, local_cols)
    stats_own = jnp.swapaxes(stats_own, 0, 1)
    grad_gathered, stats_arrived, proj_all = exchange(
        7,
        ("tensor", "gather_rows", to_half(grad_own)),
        ("tensor", "scatter", stats_own),
        ("tensor", "gather", grad_proj_part[None]),
    )
    grad_latents = grad_gathered.astype(jnp.float32)
    dmod_local = sum_blocks(stats_own, stats_arrived, tensor_index)
    cond_part = contract_lowprec("le,de->ld", to_half(dmod_local), ada_weight)
    vectors = [
        dmod_local.reshape(-1),
        grad_qv.reshape(-1),
        grad_fc1_b,
        grad_fc2_part,
        jnp.sum(proj_all[:, 0], axis=0),
    ]
    packed_all, cond_all = exchange(
        8, ("dp", "gather", jnp.concatenate(vectors)[None]), ("tensor", "gather", cond_part)
    )
    grad_conditioning = jnp.sum(cond_all, axis=0) * silu_slope(cond_f)
    packed_all = packed_all[:, 0]
    dmod_cols = lat_cap * local_cols
    dmod_all = packed_all[:, :dmod_cols].reshape(dp_count * lat_cap, local_cols)
    bias_ada = jnp.sum(dmod_all, axis=0)
    block = width // dp_count
    silu_own = lax.dynamic_slice_in_dim(
        to_half(silu_all).reshape(dp_count * lat_cap, width), dp_index * block, block, 1
    )
    summed_ada = contract_lowprec("ld,le->de", silu_own, to_half(dmod_all))
    totals = jnp.sum(packed_all[:, dmod_cols:], axis=0)
    bias_qv, bias_fc1, fc2_tot, proj_tot = jnp.split(
        totals,
        (2 * local_width, 2 * local_width + local_hidden, 2 * local_width + local_hidden + width),
    )
    bias_qv = bias_qv.reshape(2, local_width)
    return (
        block_output,
        grad_latents,
        grad_conditioning,
        summed_ada,
        bias_ada,
        summed_qkv,
        bias_qv,
        summed_proj,
        proj_tot,
        summed_fc1,
        bias_fc1,
        summed_fc2,
        fc2_tot,
    )


def solution(mesh):
    placed = (
        P("dp", None, None),
        P("dp", None),
        P("dp"),
        P(None, "tensor"),
        P("tensor"),
        P(None, None, "tensor"),
        P(None, "tensor"),
        P("tensor", None),
        P(),
        P(None, "tensor"),
        P("tensor"),
        P("tensor", None),
        P(),
        P("dp", None, None),
    )
    return jax.shard_map(
        per_device,
        mesh=mesh,
        in_specs=placed,
        out_specs=(
            P("dp", None, None),
            P("dp", None, None),
            P("dp", None),
            P("dp", "tensor"),
            P("tensor"),
            P("dp", None, "tensor"),
            P(None, "tensor"),
            P("tensor", "dp"),
            P(),
            P("dp", "tensor"),
            P("tensor"),
            P("tensor", "dp"),
            P(),
        ),
        check_vma=False,
    )
```
